256 devices in a mesh: dp: 32 (over y, z_hi, core), node: 8 (over z_lo, x).
Axes of the slice: x: 4, y: 4, z: 8 (z_hi: 4, z_lo: 2; z = z_hi * 2 + z_lo), core: 2. Of those that a mesh axis runs over, the one named last changes fastest.
Arguments:
- tokens: bfloat16 [65536, 4096], P(('dp', 'node')), may hold values from -6 to 6
- cotangent: bfloat16 [65536, 1024], P(('dp', 'node')), may hold values from -6 to 6
- quantized: bfloat16 [4096, 1024], P('dp'), may hold values from -127 to 127, as said below
- scales: float32 [4096, 4], P('dp'), may hold values from 0.0001 to 0.0004
Outputs:
- keys: bfloat16 [65536, 1024], P(('dp', 'node'))
- grad_input: bfloat16 [65536, 4096], P(('dp', 'node'))
- grad_weight: float32 [4096, 1024], P('dp', 'node')
The draws below stay inside these ranges and needn't reach their ends.
Inputs may be any that keep to these rules, and one draw needn't show every extreme that they name: `quantized`: whole numbers.
All inputs are finite; a program needn't handle non-finite values.
Results may differ from the reference program's by a relative error of at most 0.005.
Values may be sent and summed in bfloat16 or wider, within the bound.
A program may use at most 128 MiB of HBM per device.

```python
import math
import jax
import jax.numpy as jnp
from jax import lax

D = 4096
KV = 1024
BLOCK = 256
TOK_DEV = 256
TOKENS = 65536
N_DP = 32
N_NODE = 8


def draw_quantized(key, part):
    key = jax.random.fold_in(key, 11)
    codes = jax.random.randint(key, (D, KV), -127, 128)
    return codes.astype(jnp.float32).astype(jnp.bfloat16)


def block_scale(stream_key, dims, cuts, least, high):
    def one(dim, parts):
        steps = jax.random.uniform(jax.random.fold_in(jax.random.fold_in(stream_key, 6), dim), (parts,), jnp.float32, least / len(cuts), high / len(cuts))
        return jnp.repeat(jnp.exp(steps), dims[dim] // parts).reshape((-1,) + (1,) * (len(dims) - dim - 1))

    loudness = one(*cuts[0])
    for cut in cuts[1:]:
        loudness = loudness * one(*cut)
    return loudness


def gaussian(rng, extent, scale, most, cuts=(), dtype=jnp.bfloat16):
    array = scale * jax.random.normal(rng, extent, jnp.float32)
    if cuts:
        array = array * block_scale(rng, extent, cuts, -0.22, 0.18)
    return jnp.clip(array, -most, most).astype(dtype)


def setup_inputs(seed: int = 0) -> dict:
    seeds = jax.random.split(jax.random.key(seed), 5)
    return {
        "tokens": gaussian(seeds[0], (TOKENS, D), 1.0, 6.0, ((0, 256),)),
        "cotangent": gaussian(seeds[1], (TOKENS, KV), 1.0, 6.0, ((0, 256),)),
        "quantized": draw_quantized(jax.random.fold_in(seeds[4], 71), 0),
        "scales": jnp.clip(jnp.exp(math.log(0.0004) - 1.3862944 * jax.random.uniform(seeds[3], (D, KV // BLOCK), jnp.float32) ** block_scale(seeds[3], (D, KV // BLOCK), ((0, 32),), -0.2, 0.2)), 0.0001, 0.0004),
    }


def dequantize(quantized, scales):
    rows = quantized.shape[0]
    groups = scales.shape[1]
    codes = quantized.astype(jnp.float32).reshape(rows, groups, BLOCK)
    return (codes * scales[:, :, None]).reshape(rows, groups * BLOCK).astype(jnp.bfloat16)


def reference(tokens, cotangent, quantized, scales):
    weight = dequantize(quantized, scales)
    keys = jnp.dot(tokens, weight, preferred_element_type=jnp.float32).astype(jnp.bfloat16)
    grad_input = jnp.dot(cotangent, weight.T, preferred_element_type=jnp.float32).astype(jnp.bfloat16)
    token_blocks = tokens.reshape(N_DP * N_NODE, TOK_DEV, D)
    cot_blocks = cotangent.reshape(N_DP * N_NODE, TOK_DEV, KV)

    def inner(total, pair):
        block_x, block_c = pair
        return total + jnp.dot(block_x.T, block_c, preferred_element_type=jnp.float32), None

    summed, _ = lax.scan(inner, jnp.zeros((D, KV), jnp.float32), (token_blocks, cot_blocks))
    grad_weight = summed * (float(TOKENS) ** -0.5)
    return keys, grad_input, grad_weight
```

```python
import jax
import jax.numpy as jnp
from jax import lax
from jax.experimental import pallas as pl
from jax.experimental.pallas import tpu as pltpu
from jax.sharding import PartitionSpec as P

MESH = pl.DeviceIdType.MESH
BF = jnp.bfloat16
F32 = jnp.float32


def nn(a, b):
    return lax.dot_general(a, b, (((1,), (0,)), ((), ())), preferred_element_type=F32)


def nt(a, b):
    return lax.dot_general(a, b, (((1,), (1,)), ((), ())), preferred_element_type=F32)


def kernel(
    tok, cot, quantized, scales_t, keys_o, gi_o, gw_o,
    tk, ct, ctt, w1, w2, s1s, s1r, dps, dpr, s2s, s2r, xo, ys, yr, yt, zs, zr, kacc, krecv, kout, gis,
    tok_l, tok_s, tok_r, cot_l, cot_s, cot_r, key_s, key_r, key_l, gi_l, gi_s, gi_r,
    hy_s, hy_r, hz1_s, hz1_r, hz2_s, hz2_r, gz1_s, gz1_r, gz2_s, gz2_r, gy_s, gy_r,
    s1_s, s1_q, dp_s, dp_q, s2_s, s2_q, y_s, y_q, z_s, z_q,
):
    dp, node = lax.axis_index("dp"), lax.axis_index("node")
    y, zh, c = dp // 8, (dp // 2) % 4, dp % 2
    zl, x = node // 4, node % 4
    z = zh * 2 + zl
    dirz = 2 * zl - 1

    def at(dx=0, dy=0, dz=0, dc=0):
        x2, y2, z2 = (x + dx + 4) % 4, (y + dy + 4) % 4, (z + dz + 8) % 8
        c2 = c if dc == 0 else 1 - c
        return (y2 * 8 + (z2 // 2) * 2 + c2, (z2 % 2) * 4 + x2)

    sib = at(dc=1)
    pair = at(dz=0 - dirz)
    pending = []

    def send(src, dst, ss, rs, dev):
        cp = pltpu.make_async_remote_copy(src, dst, ss, rs, device_id=dev, device_id_type=MESH)
        cp.start()
        pending.append(cp)

    def arrived(dst, rs):
        pltpu.make_async_remote_copy(dst, dst, rs, rs, device_id=sib, device_id_type=MESH).wait_recv()

    def mod4(v):
        return (v + 4) % 4

    def cols(yy, h):
        return pl.ds(pl.multiple_of(((yy * 4 + h) * 2 + c) * 128, 128), 128)

    def cols_sib(yy, h):
        return pl.ds(pl.multiple_of(((yy * 4 + h) * 2 + 1 - c) * 128, 128), 128)

    cp_cot = pltpu.make_async_copy(cot, ct.at[pl.ds(0, 256)], cot_l)
    cp_cot.start()
    for i in range(4):
        yy = (y + i + 1) % 4
        for h in range(4):
            pltpu.make_async_copy(
                tok.at[:, cols(yy, h)], tk.at[yy, pl.ds(0, 256), pl.ds(h * 128, 128)], tok_l.at[i]
            ).start()

    for b in range(4):
        scale = jnp.transpose(jnp.broadcast_to(scales_t[b : b + 1, :], (128, 128)))
        for half in range(2):
            col = b * 256 + half * 128
            block = (quantized[:, col : col + 128].astype(F32) * scale).astype(BF)
            if col < 512:
                w1[y, zh, :, col : col + 128] = block
            else:
                w2[y, zh, :, col - 512 : col - 384] = block

    barrier = pltpu.get_barrier_semaphore()
    peers = [at(dx=1), at(dx=-1)] + [at(dy=o) for o in (1, 2, 3)] + [at(dz=j) for j in range(1, 8)] + [sib]
    for peer in peers:
        pl.semaphore_signal(barrier, inc=1, device_id=peer, device_id_type=MESH)
    pl.semaphore_wait(barrier, len(peers))

    send(cot, ct.at[pl.ds(256, 256)], cot_s, cot_r, sib)
    for i in range(4):
        yy = (y + i + 1) % 4
        for h in range(4):
            pltpu.make_async_remote_copy(
                tok.at[:, cols_sib(yy, h)], tk.at[yy, pl.ds(256, 256), pl.ds(h * 128, 128)],
                tok_s.at[i], tok_r.at[i], device_id=sib, device_id_type=MESH,
            ).start()

    def half(flag):
        return pl.ds(pl.multiple_of(flag * 64, 64), 64)

    def z1(w, yy, ss, rs):
        send(w.at[yy, zh], w.at[yy, zh], ss.at[0], rs.at[0], at(dz=dirz))
        send(w.at[yy, zh, half(1 - zl)], w.at[yy, zh, half(1 - zl)], ss.at[1], rs.at[1], at(dz=3 * dirz))

    def z1_arrived(w, yy, rs):
        arrived(w.at[yy, mod4(zh + dirz)], rs.at[0])
        arrived(w.at[yy, mod4(zh + 2), half(zl)], rs.at[1])

    def z2(w, yy, ss, rs):
        near, far = mod4(zh + dirz), mod4(zh + 2)
        send(w.at[yy, near], w.at[yy, near], ss.at[0], rs.at[0], pair)
        send(w.at[yy, far, half(zl)], w.at[yy, far, half(zl)], ss.at[1], rs.at[1], pair)

    def z2_arrived(w, yy, rs):
        arrived(w.at[yy, mod4(zh - dirz)], rs.at[0])
        arrived(w.at[yy, mod4(zh + 2), half(1 - zl)], rs.at[1])

    def w2_along_y(zz, role):
        for o in (1, 3, 2):
            send(w2.at[y, zz], w2.at[y, zz], gy_s.at[role, o - 1], gy_r.at[role, o - 1], at(dy=o))

    z1(w2, y, gz1_s, gz1_r)
    for o in (1, 3, 2):
        send(w1.at[y, zh], w1.at[y, zh], hy_s.at[o - 1], hy_r.at[o - 1], at(dy=o))
    z1(w1, y, hz1_s.at[0], hz1_r.at[0])
    w2_along_y(zh, 0)

    def transpose_rows(r):
        for n in range(8):
            part = ct[r * 256 : r * 256 + 256, n * 128 : n * 128 + 128]
            row = (n // 4) * 128
            ctt[n % 4, row : row + 128, r * 256 : r * 256 + 256] = jnp.transpose(part)

    cp_cot.wait()
    transpose_rows(0)
    arrived(ct.at[pl.ds(256, 256)], cot_r)
    transpose_rows(1)

    east, west = at(dx=1), at(dx=-1)
    lo, hi = pl.ds(0, 128), pl.ds(128, 128)
    xe, xw, xf = (x + 1) % 4, (x + 3) % 4, (x + 2) % 4

    for i in range(4):
        yy = (y + i + 1) % 4
        pltpu.make_async_copy(tk.at[yy, pl.ds(0, 256)], tk.at[yy, pl.ds(0, 256)], tok_l.at[i]).wait()
        arrived(tk.at[yy, pl.ds(256, 256)], tok_r.at[i])
        s1s[i] = nn(ctt[xf], tk[yy]).astype(BF)
        send(s1s.at[i, lo], s1r.at[i, lo], s1_s.at[i, 0], s1_q.at[i, 0], east)
        send(s1s.at[i, hi], s1r.at[i, hi], s1_s.at[i, 1], s1_q.at[i, 1], west)

    def x_step(i):
        yy = (y + i + 1) % 4
        right, left = nn(ctt[xe], tk[yy]), nn(ctt[xw], tk[yy])
        dps[i, 128:256] = right[128:256].astype(BF)
        dps[i, 0:128] = left[0:128].astype(BF)
        send(dps.at[i, hi], dpr.at[i, hi], dp_s.at[i, 1], dp_q.at[i, 1], east)
        send(dps.at[i, lo], dpr.at[i, lo], dp_s.at[i, 0], dp_q.at[i, 0], west)
        arrived(s1r.at[i, lo], s1_q.at[i, 0])
        s2s[i, 0:128] = (right[0:128] + s1r[i, 0:128].astype(F32)).astype(BF)
        send(s2s.at[i, lo], s2r.at[i, lo], s2_s.at[i, 0], s2_q.at[i, 0], east)
        arrived(s1r.at[i, hi], s1_q.at[i, 1])
        s2s[i, 128:256] = (left[128:256] + s1r[i, 128:256].astype(F32)).astype(BF)
        send(s2s.at[i, hi], s2r.at[i, hi], s2_s.at[i, 1], s2_q.at[i, 1], west)

    def x_end(i):
        yy = (y + i + 1) % 4
        total = nn(ctt[x], tk[yy])
        for k, rows in ((0, lo), (1, hi)):
            arrived(dpr.at[i, rows], dp_q.at[i, k])
            arrived(s2r.at[i, rows], s2_q.at[i, k])
        total = total + dpr[i].astype(F32) + s2r[i].astype(F32)
        if i < 3:
            ys[i] = total.astype(BF)
            send(ys.at[i], yr.at[i], y_s.at[i], y_q.at[i], at(dy=i + 1))
        else:
            xo[...] = total

    z1_arrived(w2, y, gz1_r)
    z2(w2, y, gz2_s, gz2_r)
    w2_along_y(mod4(zh + dirz), 1)
    for o in (1, 3, 2):
        yy = mod4(y - o)
        arrived(w1.at[yy, zh], hy_r.at[o - 1])
        z1(w1, yy, hz1_s.at[4 - o], hz1_r.at[4 - o])
    x_step(0)
    z2_arrived(w2, y, gz2_r)
    w2_along_y(mod4(zh - dirz), 2)
    w2_along_y(mod4(zh + 2), 3)
    z1_arrived(w1, y, hz1_r.at[0])
    z2(w1, y, hz2_s.at[0], hz2_r.at[0])
    x_step(1)
    for o in (1, 3):
        yy = mod4(y - o)
        z1_arrived(w1, yy, hz1_r.at[4 - o])
        z2(w1, yy, hz2_s.at[4 - o], hz2_r.at[4 - o])
    x_step(2)
    yy = mod4(y - 2)
    z1_arrived(w1, yy, hz1_r.at[2])
    z2(w1, yy, hz2_s.at[2], hz2_r.at[2])
    x_step(3)
    x_end(0)

    for r in range(4):
        z2_arrived(w1, (y + r) % 4, hz2_r.at[r])
    roles = (zh, mod4(zh + dirz), mod4(zh - dirz), mod4(zh + 2))
    for role in range(4):
        for o in (1, 3, 2):
            arrived(w2.at[mod4(y - o), roles[role]], gy_r.at[role, o - 1])

    def use_weight(p):
        a, b = w1[p].reshape(512, 512), w2[p].reshape(512, 512)
        for r in range(2):
            rows = slice(r * 256, r * 256 + 256)
            gis[p, rows] = (nt(ct[rows, 0:512], a) + nt(ct[rows, 512:1024], b)).astype(BF)
        for h in range(4):
            here = pl.ds(h * 128, 128)
            pltpu.make_async_remote_copy(
                gis.at[p, pl.ds(256, 256), here], gi_o.at[:, cols(p, h)],
                gi_s, gi_r, device_id=sib, device_id_type=MESH,
            ).start()
            pltpu.make_async_copy(gis.at[p, pl.ds(0, 256), here], gi_o.at[:, cols(p, h)], gi_l).start()
        if p == 0:
            kacc[:, 0:512] = nn(tk[p], a)
            kacc[:, 512:1024] = nn(tk[p], b)
        else:
            kacc[:, 0:512] += nn(tk[p], a)
            kacc[:, 512:1024] += nn(tk[p], b)

    use_weight(0)
    x_end(1)
    use_weight(1)
    x_end(2)
    use_weight(2)
    x_end(3)
    for i in range(3):
        arrived(yr.at[i], y_q.at[i])
    total = xo[...] + yr[0].astype(F32) + yr[1].astype(F32) + yr[2].astype(F32)
    for b in range(8):
        block = total[(b % 2) * 128 : (b % 2) * 128 + 128, (b // 2) * 128 : (b // 2) * 128 + 128]
        yt[b] = block
        zs[b] = block.astype(BF)
    for j in (4, 3, 5, 2, 6, 1, 7):
        send(zs.at[(z + j) % 8], zr.at[j - 1], z_s.at[j - 1], z_q.at[j - 1], at(dz=j))
    use_weight(3)
    send(kacc.at[pl.ds(256, 256)], krecv, key_s, key_r, sib)
    for j in (1, 7, 2, 6, 3, 5, 4):
        arrived(zr.at[j - 1], z_q.at[j - 1])
    acc = yt[z]
    for j in range(7):
        acc = acc + zr[j].astype(F32)
    gw_o[...] = jnp.transpose(acc) * 0.00390625
    arrived(krecv, key_r)
    kout[...] = (kacc[0:256] + krecv[...]).astype(BF)
    cp_key = pltpu.make_async_copy(kout, keys_o, key_l)
    cp_key.start()

    for cp in pending:
        cp.wait_send()
    for i in range(4):
        pltpu.make_async_copy(tk.at[0, pl.ds(256, 256)], tk.at[0, pl.ds(256, 256)], tok_s.at[i]).wait()
    wide = pl.ds(0, 2048)
    pltpu.make_async_copy(gi_o.at[:, wide], gi_o.at[:, wide], gi_l).wait()
    pltpu.make_async_copy(gi_o.at[:, wide], gi_o.at[:, wide], gi_s).wait()
    pltpu.make_async_copy(gi_o.at[:, wide], gi_o.at[:, wide], gi_r).wait()
    cp_key.wait()


def shards(tokens, cotangent, quantized, scales):
    dma = pltpu.SemaphoreType.DMA
    vm = pltpu.VMEM
    piece = (4, 256, 512)
    scratch = [
        vm((4, 512, 512), BF), vm((512, 1024), BF), vm((4, 256, 512), BF),
        vm((4, 4, 128, 512), BF), vm((4, 4, 128, 512), BF),
        vm(piece, BF), vm(piece, BF), vm(piece, BF), vm(piece, BF), vm(piece, BF), vm(piece, BF),
        vm((256, 512), F32), vm((3, 256, 512), BF), vm((3, 256, 512), BF),
        vm((8, 128, 128), F32), vm((8, 128, 128), BF), vm((7, 128, 128), BF),
        vm((512, 1024), F32), vm((256, 1024), F32), vm((256, 1024), BF), vm((4, 512, 512), BF),
        dma((4,)), dma((4,)), dma((4,)), dma, dma, dma, dma, dma, dma, dma, dma, dma,
        dma((3,)), dma((3,)), dma((4, 2)), dma((4, 2)), dma((4, 2)), dma((4, 2)),
        dma((2,)), dma((2,)), dma((2,)), dma((2,)), dma((4, 3)), dma((4, 3)),
        dma((4, 2)), dma((4, 2)), dma((4, 2)), dma((4, 2)), dma((4, 2)), dma((4, 2)),
        dma((3,)), dma((3,)), dma((7,)), dma((7,)),
    ]
    anywhere = pl.BlockSpec(memory_space=pl.ANY)
    vmem = pl.BlockSpec(memory_space=pltpu.VMEM)
    return pl.pallas_call(
        kernel,
        out_shape=(
            jax.ShapeDtypeStruct((256, 1024), BF),
            jax.ShapeDtypeStruct((256, 4096), BF),
            jax.ShapeDtypeStruct((128, 128), F32),
        ),
        in_specs=[anywhere, anywhere, vmem, vmem],
        out_specs=(anywhere, anywhere, vmem),
        scratch_shapes=scratch,
        compiler_params=pltpu.CompilerParams(
            collective_id=0, has_side_effects=True, vmem_limit_bytes=48 * 2**20
        ),
        cost_estimate=pl.CostEstimate(flops=6442450944, bytes_accessed=8 * 2**20, transcendentals=0),
        name="key_projection",
    )(tokens, cotangent, quantized, scales.T)


def solution(mesh):
    in_specs = (P(("dp", "node"), None), P(("dp", "node"), None), P("dp", None), P("dp", None))
    out_specs = (P(("dp", "node"), None), P(("dp", "node"), None), P("dp", "node"))
    return jax.shard_map(shards, mesh=mesh, in_specs=in_specs, out_specs=out_specs, check_vma=False)
```

```python
import jax
import jax.numpy as jnp
from jax import lax
from jax.experimental import pallas as pl
from jax.experimental.pallas import tpu as pltpu
from jax.sharding import PartitionSpec as P

MESH = pl.DeviceIdType.MESH
BF = jnp.bfloat16
F32 = jnp.float32


def nn(a, b):
    return lax.dot_general(a, b, (((1,), (0,)), ((), ())), preferred_element_type=F32)


def nt(a, b):
    return lax.dot_general(a, b, (((1,), (1,)), ((), ())), preferred_element_type=F32)


def kernel(
    tok, cot, quantized, scales_t, keys_o, gi_o, gw_o,
    tk, ct, ctt, w1, w2, s1s, s1r, dps, dpr, s2s, s2r, xo, ys, yr, yt, zs, zr, kacc, krecv, kout, gis,
    tok_l, tok_s, tok_r, cot_l, cot_s, cot_r, key_s, key_r, key_l, gi_l, gi_s, gi_r,
    hy_s, hy_r, hz_s, hz_r, gz_s, gz_r, gy_s, gy_r,
    s1_s, s1_q, dp_s, dp_q, s2_s, s2_q, y_s, y_q, z_s, z_q,
):
    dp, node = lax.axis_index("dp"), lax.axis_index("node")
    y, zh, c = dp // 8, (dp // 2) % 4, dp % 2
    zl, x = node // 4, node % 4
    z = zh * 2 + zl
    dirz = 2 * zl - 1

    def at(dx=0, dy=0, dz=0, dc=0):
        x2, y2, z2 = (x + dx + 4) % 4, (y + dy + 4) % 4, (z + dz + 8) % 8
        c2 = c if dc == 0 else 1 - c
        return (y2 * 8 + (z2 // 2) * 2 + c2, (z2 % 2) * 4 + x2)

    sib = at(dc=1)
    pending = []

    def send(src, dst, ss, rs, dev):
        cp = pltpu.make_async_remote_copy(src, dst, ss, rs, device_id=dev, device_id_type=MESH)
        cp.start()
        pending.append(cp)

    def arrived(dst, rs):
        pltpu.make_async_remote_copy(dst, dst, rs, rs, device_id=sib, device_id_type=MESH).wait_recv()

    def mod4(v):
        return (v + 4) % 4

    def cols(yy, h):
        return pl.ds(pl.multiple_of(((yy * 4 + h) * 2 + c) * 128, 128), 128)

    def cols_sib(yy, h):
        return pl.ds(pl.multiple_of(((yy * 4 + h) * 2 + 1 - c) * 128, 128), 128)

    cp_cot = pltpu.make_async_copy(cot, ct.at[pl.ds(0, 256)], cot_l)
    cp_cot.start()
    for i in range(4):
        yy = (y + i + 1) % 4
        for h in range(4):
            pltpu.make_async_copy(
                tok.at[:, cols(yy, h)], tk.at[yy, pl.ds(0, 256), pl.ds(h * 128, 128)], tok_l.at[i]
            ).start()

    for b in range(4):
        scale = jnp.transpose(jnp.broadcast_to(scales_t[b : b + 1, :], (128, 128)))
        for half in range(2):
            col = b * 256 + half * 128
            block = (quantized[:, col : col + 128].astype(F32) * scale).astype(BF)
            if col < 512:
                w1[y, zh, :, col : col + 128] = block
            else:
                w2[y, zh, :, col - 512 : col - 384] = block

    barrier = pltpu.get_barrier_semaphore()
    peers = [at(dx=1), at(dx=-1)] + [at(dy=o) for o in (1, 2, 3)] + [at(dz=j) for j in range(1, 8)] + [sib]
    for peer in peers:
        pl.semaphore_signal(barrier, inc=1, device_id=peer, device_id_type=MESH)
    pl.semaphore_wait(barrier, len(peers))

    send(cot, ct.at[pl.ds(256, 256)], cot_s, cot_r, sib)
    for i in range(4):
        yy = (y + i + 1) % 4
        for h in range(4):
            pltpu.make_async_remote_copy(
                tok.at[:, cols_sib(yy, h)], tk.at[yy, pl.ds(256, 256), pl.ds(h * 128, 128)],
                tok_s.at[i], tok_r.at[i], device_id=sib, device_id_type=MESH,
            ).start()

    def half(flag):
        return pl.ds(pl.multiple_of(flag * 64, 64), 64)

    cross, pair = at(dz=dirz), at(dz=0 - dirz)
    near, back, far = mod4(zh + dirz), mod4(zh - dirz), mod4(zh + 2)

    def z_send(w, yy, phase, ss, rs):
        block, dev = (
            (w.at[yy, zh], cross),
            (w.at[yy, near], pair),
            (w.at[yy, back, half(1 - zl)], cross),
            (w.at[yy, far, half(zl)], pair),
        )[phase]
        send(block, block, ss.at[phase], rs.at[phase], dev)

    def z_wait(w, yy, phase, rs):
        block = (w.at[yy, near], w.at[yy, back], w.at[yy, far, half(zl)], w.at[yy, far, half(1 - zl)])[phase]
        arrived(block, rs.at[phase])

    def h_send(r, phase):
        z_send(w1, (y + r) % 4, phase, hz_s.at[r], hz_r.at[r])

    def h_pass(r, phase):
        z_wait(w1, (y + r) % 4, phase, hz_r.at[r])
        if phase < 3:
            h_send(r, phase + 1)

    def h_first(o):
        yy = mod4(y - o)
        arrived(w1.at[yy, zh], hy_r.at[o - 1])
        h_send(4 - o, 0)

    roles = (
        (zh, pl.ds(0, 128)), (near, pl.ds(0, 128)), (back, pl.ds(0, 128)), (far, half(zl)), (far, half(1 - zl)),
    )

    def g_along_y(role):
        zz, rows = roles[role]
        for o in (1, 3, 2):
            send(w2.at[y, zz, rows], w2.at[y, zz, rows], gy_s.at[role, o - 1], gy_r.at[role, o - 1], at(dy=o))

    def g_pass(phase):
        z_wait(w2, y, phase, gz_r)
        if phase < 3:
            z_send(w2, y, phase + 1, gz_s, gz_r)
        g_along_y(phase + 1)

    z_send(w2, y, 0, gz_s, gz_r)
    for o in (1, 3, 2):
        send(w1.at[y, zh], w1.at[y, zh], hy_s.at[o - 1], hy_r.at[o - 1], at(dy=o))
    h_send(0, 0)
    g_along_y(0)

    def transpose_rows(r):
        for n in range(8):
            part = ct[r * 256 : r * 256 + 256, n * 128 : n * 128 + 128]
            row = (n // 4) * 128
            ctt[n % 4, row : row + 128, r * 256 : r * 256 + 256] = jnp.transpose(part)

    cp_cot.wait()
    transpose_rows(0)
    arrived(ct.at[pl.ds(256, 256)], cot_r)
    transpose_rows(1)

    east, west = at(dx=1), at(dx=-1)
    lo, hi = pl.ds(0, 128), pl.ds(128, 128)
    xe, xw, xf = (x + 1) % 4, (x + 3) % 4, (x + 2) % 4

    def put(ref, i, rows, value):
        for q in range(4):
            ref[i, q, rows] = value[:, q * 128 : q * 128 + 128].astype(ref.dtype)

    def get(ref, i, rows):
        return jnp.concatenate([ref[i, q, rows].astype(F32) for q in range(4)], axis=1)

    top, low = slice(0, 128), slice(128, 256)

    def tokens_of(yy, q):
        return tk[yy, :, pl.ds(pl.multiple_of(((zh + q + 1) % 4) * 128, 128), 128)]

    def chunk(yy):
        return jnp.concatenate([tokens_of(yy, q) for q in range(4)], axis=1)

    def s1(i):
        yy = (y + i + 1) % 4
        pltpu.make_async_copy(tk.at[yy, pl.ds(0, 256)], tk.at[yy, pl.ds(0, 256)], tok_l.at[i]).wait()
        arrived(tk.at[yy, pl.ds(256, 256)], tok_r.at[i])
        put(s1s, i, slice(0, 256), nn(ctt[xf], chunk(yy)))
        send(s1s.at[i, :, lo], s1r.at[i, :, lo], s1_s.at[i, 0], s1_q.at[i, 0], east)
        send(s1s.at[i, :, hi], s1r.at[i, :, hi], s1_s.at[i, 1], s1_q.at[i, 1], west)

    def pieces(i):
        return ((i, slice(None)),) if i < 3 else tuple((3 + q, q) for q in range(4))

    def x_step(i):
        tokens = chunk((y + i + 1) % 4)
        right, left = nn(ctt[xe], tokens), nn(ctt[xw], tokens)
        put(dps, i, low, right[128:256])
        put(dps, i, top, left[0:128])
        arrived(s1r.at[i, :, lo], s1_q.at[i, 0])
        put(s2s, i, top, right[0:128] + get(s1r, i, top))
        arrived(s1r.at[i, :, hi], s1_q.at[i, 1])
        put(s2s, i, low, left[128:256] + get(s1r, i, low))
        for k, q in pieces(i):
            send(s2s.at[i, q, lo], s2r.at[i, q, lo], s2_s.at[k, 0], s2_q.at[k, 0], east)
            send(s2s.at[i, q, hi], s2r.at[i, q, hi], s2_s.at[k, 1], s2_q.at[k, 1], west)
            send(dps.at[i, q, hi], dpr.at[i, q, hi], dp_s.at[k, 1], dp_q.at[k, 1], east)
            send(dps.at[i, q, lo], dpr.at[i, q, lo], dp_s.at[k, 0], dp_q.at[k, 0], west)

    def x_wait(i, k, q):
        for j, rows in ((0, lo), (1, hi)):
            arrived(s2r.at[i, q, rows], s2_q.at[k, j])
            arrived(dpr.at[i, q, rows], dp_q.at[k, j])

    def x_end(i):
        total = nn(ctt[x], chunk((y + i + 1) % 4))
        x_wait(i, i, slice(None))
        both = slice(0, 256)
        put(ys, i, both, total + get(dpr, i, both) + get(s2r, i, both))
        for q in range(4):
            send(ys.at[i, q], yr.at[i, q], y_s.at[i, q], y_q.at[i, q], at(dy=i + 1))

    def own_chunk():
        total = nn(ctt[x], chunk(y))
        for q in range(4):
            xo[q] = total[:, q * 128 : q * 128 + 128]

    def last(q):
        total = xo[q]
        x_wait(3, 3 + q, q)
        total = total + dpr[3, q].astype(F32) + s2r[3, q].astype(F32)
        for i in range(3):
            arrived(yr.at[i, q], y_q.at[i, q])
            total = total + yr[i, q].astype(F32)
        zs[q, 0] = total[0:128].astype(BF)
        zs[q, 1] = total[128:256].astype(BF)
        if q < 3:
            for t in range(2):
                dz = 2 * (q + 1) + t - zl
                send(zs.at[q, t], zr.at[q * 2 + zl], z_s.at[q * 2 + t], z_q.at[q * 2 + zl], at(dz=dz))
        else:
            send(zs.at[q, 1 - zl], zr.at[6], z_s.at[6], z_q.at[6], pair)
            yt[0] = total[0:128]
            yt[1] = total[128:256]

    for i in range(4):
        s1(i)
    g_pass(0)
    h_first(1)
    h_first(3)
    h_pass(0, 0)
    x_step(0)
    g_pass(1)
    h_first(2)
    h_pass(0, 1)
    h_pass(3, 0)
    h_pass(1, 0)
    x_step(1)
    g_pass(2)
    h_pass(0, 2)
    h_pass(3, 1)
    h_pass(1, 1)
    h_pass(2, 0)
    x_step(2)
    g_pass(3)
    h_pass(3, 2)
    h_pass(1, 2)
    h_pass(2, 1)
    x_step(3)
    h_pass(2, 2)
    x_end(0)

    for r in range(4):
        h_pass(r, 3)
    for role in range(5):
        zz, rows = roles[role]
        for o in (1, 3, 2):
            arrived(w2.at[mod4(y - o), zz, rows], gy_r.at[role, o - 1])

    def use_weight(p):
        a, b = w1[p].reshape(512, 512), w2[p].reshape(512, 512)
        for r in range(2):
            rows = slice(r * 256, r * 256 + 256)
            gis[p, rows] = (nt(ct[rows, 0:512], a) + nt(ct[rows, 512:1024], b)).astype(BF)
        for h in range(4):
            here = pl.ds(h * 128, 128)
            pltpu.make_async_remote_copy(
                gis.at[p, pl.ds(256, 256), here], gi_o.at[:, cols(p, h)],
                gi_s, gi_r, device_id=sib, device_id_type=MESH,
            ).start()
            pltpu.make_async_copy(gis.at[p, pl.ds(0, 256), here], gi_o.at[:, cols(p, h)], gi_l).start()
        if p == 0:
            kacc[:, 0:512] = nn(tk[p], a)
            kacc[:, 512:1024] = nn(tk[p], b)
        else:
            kacc[:, 0:512] += nn(tk[p], a)
            kacc[:, 512:1024] += nn(tk[p], b)

    use_weight(0)
    x_end(1)
    use_weight(1)
    use_weight(2)
    x_end(2)
    use_weight(3)
    send(kacc.at[pl.ds(256, 256)], krecv, key_s, key_r, sib)
    own_chunk()
    for q in range(4):
        last(q)
    acc = yt[zl]
    for j in range(7):
        arrived(zr.at[j], z_q.at[j])
        acc = acc + zr[j].astype(F32)
    gw_o[...] = jnp.transpose(acc) * 0.00390625
    arrived(krecv, key_r)
    kout[...] = (kacc[0:256] + krecv[...]).astype(BF)
    cp_key = pltpu.make_async_copy(kout, keys_o, key_l)
    cp_key.start()

    for cp in pending:
        cp.wait_send()
    for i in range(4):
        pltpu.make_async_copy(tk.at[0, pl.ds(256, 256)], tk.at[0, pl.ds(256, 256)], tok_s.at[i]).wait()
    wide = pl.ds(0, 2048)
    pltpu.make_async_copy(gi_o.at[:, wide], gi_o.at[:, wide], gi_l).wait()
    pltpu.make_async_copy(gi_o.at[:, wide], gi_o.at[:, wide], gi_s).wait()
    pltpu.make_async_copy(gi_o.at[:, wide], gi_o.at[:, wide], gi_r).wait()
    cp_key.wait()


def shards(tokens, cotangent, quantized, scales):
    dma = pltpu.SemaphoreType.DMA
    vm = pltpu.VMEM
    piece = (4, 4, 256, 128)
    scratch = [
        vm((4, 512, 512), BF), vm((512, 1024), BF), vm((4, 256, 512), BF),
        vm((4, 4, 128, 512), BF), vm((4, 4, 128, 512), BF),
        vm(piece, BF), vm(piece, BF), vm(piece, BF), vm(piece, BF), vm(piece, BF), vm(piece, BF),
        vm((4, 256, 128), F32), vm((3, 4, 256, 128), BF), vm((3, 4, 256, 128), BF),
        vm((2, 128, 128), F32), vm((4, 2, 128, 128), BF), vm((7, 128, 128), BF),
        vm((512, 1024), F32), vm((256, 1024), F32), vm((256, 1024), BF), vm((4, 512, 512), BF),
        dma((4,)), dma((4,)), dma((4,)), dma, dma, dma, dma, dma, dma, dma, dma, dma,
        dma((3,)), dma((3,)), dma((4, 4)), dma((4, 4)), dma((4,)), dma((4,)), dma((5, 3)), dma((5, 3)),
        dma((4, 2)), dma((4, 2)), dma((7, 2)), dma((7, 2)), dma((7, 2)), dma((7, 2)),
        dma((3, 4)), dma((3, 4)), dma((7,)), dma((7,)),
    ]
    anywhere = pl.BlockSpec(memory_space=pl.ANY)
    hbm = pl.BlockSpec(memory_space=pltpu.HBM)
    vmem = pl.BlockSpec(memory_space=pltpu.VMEM)
    return pl.pallas_call(
        kernel,
        out_shape=(
            jax.ShapeDtypeStruct((256, 1024), BF),
            jax.ShapeDtypeStruct((256, 4096), BF),
            jax.ShapeDtypeStruct((128, 128), F32),
        ),
        in_specs=[hbm, hbm, vmem, vmem],
        out_specs=(anywhere, anywhere, vmem),
        scratch_shapes=scratch,
        compiler_params=pltpu.CompilerParams(
            collective_id=0, has_side_effects=True, vmem_limit_bytes=48 * 2**20
        ),
        cost_estimate=pl.CostEstimate(flops=6442450944, bytes_accessed=8 * 2**20, transcendentals=0),
        name="key_projection",
    )(tokens, cotangent, quantized, scales.T)


def solution(mesh):
    in_specs = (P(("dp", "node"), None), P(("dp", "node"), None), P("dp", None), P("dp", None))
    out_specs = (P(("dp", "node"), None), P(("dp", "node"), None), P("dp", "node"))
    return jax.shard_map(shards, mesh=mesh, in_specs=in_specs, out_specs=out_specs, check_vma=False)
```

```python
import jax
import jax.numpy as jnp
from jax import lax
from jax.experimental import pallas as pl
from jax.experimental.pallas import tpu as pltpu
from jax.sharding import PartitionSpec as P

MESH = pl.DeviceIdType.MESH
BF = jnp.bfloat16
F32 = jnp.float32


def nn(a, b):
    return lax.dot_general(a, b, (((1,), (0,)), ((), ())), preferred_element_type=F32)


def nt(a, b):
    return lax.dot_general(a, b, (((1,), (1,)), ((), ())), preferred_element_type=F32)


def kernel(
    tok, cot, codes_h, scales_h, keys_o, gi_o, gw_o,
    quantized, scales_t, tk, ct, ctt, w1, w2, s1s, s1r, dps, dpr, s2s, s2r, xo, ys, yr, yt, zs, zr, kacc, krecv, kout, gis,
    codes_l, scales_l, tok_l, tok_s, tok_r, cot_l, cot_s, cot_r, key_s, key_r, key_l, gi_l, gi_s, gi_r,
    hy_s, hy_r, hz_s, hz_r, gz_s, gz_r, gy_s, gy_r,
    s1_s, s1_q, dp_s, dp_q, s2_s, s2_q, y_s, y_q, z_s, z_q,
):
    dp, node = lax.axis_index("dp"), lax.axis_index("node")
    y, zh, c = dp // 8, (dp // 2) % 4, dp % 2
    zl, x = node // 4, node % 4
    z = zh * 2 + zl
    dirz = 2 * zl - 1

    def at(dx=0, dy=0, dz=0, dc=0):
        x2, y2, z2 = (x + dx + 4) % 4, (y + dy + 4) % 4, (z + dz + 8) % 8
        c2 = c if dc == 0 else 1 - c
        return (y2 * 8 + (z2 // 2) * 2 + c2, (z2 % 2) * 4 + x2)

    sib = at(dc=1)
    pending = []

    def send(src, dst, ss, rs, dev):
        cp = pltpu.make_async_remote_copy(src, dst, ss, rs, device_id=dev, device_id_type=MESH)
        cp.start()
        pending.append(cp)

    def arrived(dst, rs):
        pltpu.make_async_remote_copy(dst, dst, rs, rs, device_id=sib, device_id_type=MESH).wait_recv()

    def mod4(v):
        return (v + 4) % 4

    barrier = pltpu.get_barrier_semaphore()
    peers = [at(dx=1), at(dx=-1)] + [at(dy=o) for o in (1, 2, 3)] + [at(dz=j) for j in range(1, 8)] + [sib]
    for peer in peers:
        pl.semaphore_signal(barrier, inc=1, device_id=peer, device_id_type=MESH)

    def cols(yy, h):
        return pl.ds(pl.multiple_of(((yy * 4 + h) * 2 + c) * 128, 128), 128)

    def cols_sib(yy, h):
        return pl.ds(pl.multiple_of(((yy * 4 + h) * 2 + 1 - c) * 128, 128), 128)

    cp_cot = pltpu.make_async_copy(cot, ct.at[pl.ds(0, 256)], cot_l)
    cp_cot.start()
    cp_scales = pltpu.make_async_copy(scales_h, scales_t, scales_l)
    cp_scales.start()
    cp_codes = pltpu.make_async_copy(codes_h, quantized, codes_l)
    cp_codes.start()
    for i in range(4):
        yy = (y + i + 1) % 4
        for h in range(4):
            pltpu.make_async_copy(
                tok.at[:, cols(yy, h)], tk.at[yy, pl.ds(0, 256), pl.ds(h * 128, 128)], tok_l.at[i]
            ).start()

    cp_scales.wait()
    cp_codes.wait()
    for b in range(4):
        scale = jnp.transpose(jnp.broadcast_to(scales_t[b : b + 1, :], (128, 128)))
        for half in range(2):
            col = b * 256 + half * 128
            block = (quantized[:, col : col + 128].astype(F32) * scale).astype(BF)
            if col < 512:
                w1[y, zh, :, col : col + 128] = block
            else:
                w2[y, zh, :, col - 512 : col - 384] = block

    pl.semaphore_wait(barrier, len(peers))

    send(cot, ct.at[pl.ds(256, 256)], cot_s, cot_r, sib)
    for i in range(4):
        yy = (y + i + 1) % 4
        for h in range(4):
            pltpu.make_async_remote_copy(
                tok.at[:, cols_sib(yy, h)], tk.at[yy, pl.ds(256, 256), pl.ds(h * 128, 128)],
                tok_s.at[i], tok_r.at[i], device_id=sib, device_id_type=MESH,
            ).start()

    def half(flag):
        return pl.ds(pl.multiple_of(flag * 64, 64), 64)

    cross, pair = at(dz=dirz), at(dz=0 - dirz)
    near, back, far = mod4(zh + dirz), mod4(zh - dirz), mod4(zh + 2)

    def z_send(w, yy, phase, ss, rs):
        block, dev = (
            (w.at[yy, zh], cross),
            (w.at[yy, near], pair),
            (w.at[yy, back, half(1 - zl)], cross),
            (w.at[yy, far, half(zl)], pair),
        )[phase]
        send(block, block, ss.at[phase], rs.at[phase], dev)

    def z_wait(w, yy, phase, rs):
        block = (w.at[yy, near], w.at[yy, back], w.at[yy, far, half(zl)], w.at[yy, far, half(1 - zl)])[phase]
        arrived(block, rs.at[phase])

    def h_send(r, phase):
        z_send(w1, (y + r) % 4, phase, hz_s.at[r], hz_r.at[r])

    def h_pass(r, phase):
        z_wait(w1, (y + r) % 4, phase, hz_r.at[r])
        if phase < 3:
            h_send(r, phase + 1)

    def h_first(o):
        yy = mod4(y - o)
        arrived(w1.at[yy, zh], hy_r.at[o - 1])
        h_send(4 - o, 0)

    roles = (
        (zh, pl.ds(0, 128)), (near, pl.ds(0, 128)), (back, pl.ds(0, 128)), (far, half(zl)), (far, half(1 - zl)),
    )

    def g_along_y(role):
        zz, rows = roles[role]
        for o in (1, 3, 2):
            send(w2.at[y, zz, rows], w2.at[y, zz, rows], gy_s.at[role, o - 1], gy_r.at[role, o - 1], at(dy=o))

    def g_pass(phase):
        z_wait(w2, y, phase, gz_r)
        if phase < 3:
            z_send(w2, y, phase + 1, gz_s, gz_r)
        g_along_y(phase + 1)

    z_send(w2, y, 0, gz_s, gz_r)
    for o in (1, 3, 2):
        send(w1.at[y, zh], w1.at[y, zh], hy_s.at[o - 1], hy_r.at[o - 1], at(dy=o))
    h_send(0, 0)
    g_along_y(0)

    def transpose_rows(r):
        for n in range(8):
            part = ct[r * 256 : r * 256 + 256, n * 128 : n * 128 + 128]
            row = (n // 4) * 128
            ctt[n % 4, row : row + 128, r * 256 : r * 256 + 256] = jnp.transpose(part)

    cp_cot.wait()
    transpose_rows(0)
    arrived(ct.at[pl.ds(256, 256)], cot_r)
    transpose_rows(1)

    east, west = at(dx=1), at(dx=-1)
    lo, hi = pl.ds(0, 128), pl.ds(128, 128)
    xe, xw, xf = (x + 1) % 4, (x + 3) % 4, (x + 2) % 4

    def put(ref, i, rows, value):
        for q in range(4):
            ref[i, q, rows] = value[:, q * 128 : q * 128 + 128].astype(ref.dtype)

    def get(ref, i, rows):
        return jnp.concatenate([ref[i, q, rows].astype(F32) for q in range(4)], axis=1)

    top, low = slice(0, 128), slice(128, 256)

    def tokens_of(yy, q):
        return tk[yy, :, pl.ds(pl.multiple_of(((zh + q + 1) % 4) * 128, 128), 128)]

    def chunk(yy):
        return jnp.concatenate([tokens_of(yy, q) for q in range(4)], axis=1)

    def s1(i):
        yy = (y + i + 1) % 4
        pltpu.make_async_copy(tk.at[yy, pl.ds(0, 256)], tk.at[yy, pl.ds(0, 256)], tok_l.at[i]).wait()
        arrived(tk.at[yy, pl.ds(256, 256)], tok_r.at[i])
        put(s1s, i, slice(0, 256), nn(ctt[xf], chunk(yy)))
        send(s1s.at[i, :, lo], s1r.at[i, :, lo], s1_s.at[i, 0], s1_q.at[i, 0], east)
        send(s1s.at[i, :, hi], s1r.at[i, :, hi], s1_s.at[i, 1], s1_q.at[i, 1], west)

    def pieces(i):
        return ((i, slice(None)),) if i < 2 else tuple((4 * i - 6 + q, q) for q in range(4))

    def x_step(i):
        tokens = chunk((y + i + 1) % 4)
        right, left = nn(ctt[xe], tokens), nn(ctt[xw], tokens)
        put(dps, i, low, right[128:256])
        put(dps, i, top, left[0:128])
        arrived(s1r.at[i, :, lo], s1_q.at[i, 0])
        put(s2s, i, top, right[0:128] + get(s1r, i, top))
        arrived(s1r.at[i, :, hi], s1_q.at[i, 1])
        put(s2s, i, low, left[128:256] + get(s1r, i, low))
        for k, q in pieces(i):
            send(s2s.at[i, q, lo], s2r.at[i, q, lo], s2_s.at[k, 0], s2_q.at[k, 0], east)
            send(s2s.at[i, q, hi], s2r.at[i, q, hi], s2_s.at[k, 1], s2_q.at[k, 1], west)
            send(dps.at[i, q, hi], dpr.at[i, q, hi], dp_s.at[k, 1], dp_q.at[k, 1], east)
            send(dps.at[i, q, lo], dpr.at[i, q, lo], dp_s.at[k, 0], dp_q.at[k, 0], west)

    def x_wait(i, k, q):
        for j, rows in ((0, lo), (1, hi)):
            arrived(s2r.at[i, q, rows], s2_q.at[k, j])
            arrived(dpr.at[i, q, rows], dp_q.at[k, j])

    def x_end(i):
        total = nn(ctt[x], chunk((y + i + 1) % 4))
        if i < 2:
            x_wait(i, i, slice(None))
        for q in range(4):
            if i == 2:
                x_wait(i, 2 + q, q)
            piece = total[:, q * 128 : q * 128 + 128]
            ys[i, q] = (piece + dpr[i, q].astype(F32) + s2r[i, q].astype(F32)).astype(BF)
            send(ys.at[i, q], yr.at[i, q], y_s.at[i, q], y_q.at[i, q], at(dy=i + 1))

    def own_chunk():
        total = nn(ctt[x], chunk(y))
        for q in range(4):
            xo[q] = total[:, q * 128 : q * 128 + 128]

    def last(q):
        total = xo[q]
        x_wait(3, 6 + q, q)
        total = total + dpr[3, q].astype(F32) + s2r[3, q].astype(F32)
        for i in range(3):
            arrived(yr.at[i, q], y_q.at[i, q])
            total = total + yr[i, q].astype(F32)
        zs[q, 0] = total[0:128].astype(BF)
        zs[q, 1] = total[128:256].astype(BF)
        if q < 3:
            for t in range(2):
                dz = 2 * (q + 1) + t - zl
                send(zs.at[q, t], zr.at[q * 2 + zl], z_s.at[q * 2 + t], z_q.at[q * 2 + zl], at(dz=dz))
        else:
            send(zs.at[q, 1 - zl], zr.at[6], z_s.at[6], z_q.at[6], pair)
            yt[0] = total[0:128]
            yt[1] = total[128:256]

    for i in range(4):
        s1(i)
    g_pass(0)
    h_first(1)
    h_first(3)
    h_pass(0, 0)
    x_step(0)
    g_pass(1)
    h_first(2)
    h_pass(0, 1)
    h_pass(3, 0)
    h_pass(1, 0)
    x_step(1)
    g_pass(2)
    h_pass(0, 2)
    h_pass(3, 1)
    h_pass(1, 1)
    h_pass(2, 0)
    x_step(2)
    g_pass(3)
    h_pass(3, 2)
    h_pass(1, 2)
    h_pass(2, 1)
    x_step(3)
    h_pass(2, 2)
    x_end(0)
    x_end(1)

    for r in range(4):
        h_pass(r, 3)
    for role in range(5):
        zz, rows = roles[role]
        for o in (1, 3, 2):
            arrived(w2.at[mod4(y - o), zz, rows], gy_r.at[role, o - 1])

    def use_weight(p):
        a, b = w1[p].reshape(512, 512), w2[p].reshape(512, 512)
        for r in range(2):
            rows = slice(r * 256, r * 256 + 256)
            gis[p, rows] = (nt(ct[rows, 0:512], a) + nt(ct[rows, 512:1024], b)).astype(BF)
        for h in range(4):
            here = pl.ds(h * 128, 128)
            pltpu.make_async_remote_copy(
                gis.at[p, pl.ds(256, 256), here], gi_o.at[:, cols(p, h)],
                gi_s, gi_r, device_id=sib, device_id_type=MESH,
            ).start()
            pltpu.make_async_copy(gis.at[p, pl.ds(0, 256), here], gi_o.at[:, cols(p, h)], gi_l).start()
        if p == 0:
            kacc[:, 0:512] = nn(tk[p], a)
            kacc[:, 512:1024] = nn(tk[p], b)
        else:
            kacc[:, 0:512] += nn(tk[p], a)
            kacc[:, 512:1024] += nn(tk[p], b)

    use_weight(0)
    use_weight(1)
    x_end(2)
    use_weight(2)
    use_weight(3)
    send(kacc.at[pl.ds(256, 256)], krecv, key_s, key_r, sib)
    own_chunk()
    for q in range(4):
        last(q)
    acc = yt[zl]
    for j in range(7):
        arrived(zr.at[j], z_q.at[j])
        acc = acc + zr[j].astype(F32)
    gw_o[...] = jnp.transpose(acc) * 0.00390625
    arrived(krecv, key_r)
    kout[...] = (kacc[0:256] + krecv[...]).astype(BF)
    cp_key = pltpu.make_async_copy(kout, keys_o, key_l)
    cp_key.start()

    for cp in pending:
        cp.wait_send()
    for i in range(4):
        pltpu.make_async_copy(tk.at[0, pl.ds(256, 256)], tk.at[0, pl.ds(256, 256)], tok_s.at[i]).wait()
    wide = pl.ds(0, 2048)
    pltpu.make_async_copy(gi_o.at[:, wide], gi_o.at[:, wide], gi_l).wait()
    pltpu.make_async_copy(gi_o.at[:, wide], gi_o.at[:, wide], gi_s).wait()
    pltpu.make_async_copy(gi_o.at[:, wide], gi_o.at[:, wide], gi_r).wait()
    cp_key.wait()


def shards(tokens, cotangent, quantized, scales):
    dma = pltpu.SemaphoreType.DMA
    vm = pltpu.VMEM
    piece = (4, 4, 256, 128)
    scratch = [
        vm((128, 1024), BF), vm((4, 128), F32), vm((4, 512, 512), BF), vm((512, 1024), BF), vm((4, 256, 512), BF),
        vm((4, 4, 128, 512), BF), vm((4, 4, 128, 512), BF),
        vm(piece, BF), vm(piece, BF), vm(piece, BF), vm(piece, BF), vm(piece, BF), vm(piece, BF),
        vm((4, 256, 128), F32), vm((3, 4, 256, 128), BF), vm((3, 4, 256, 128), BF),
        vm((2, 128, 128), F32), vm((4, 2, 128, 128), BF), vm((7, 128, 128), BF),
        vm((512, 1024), F32), vm((256, 1024), F32), vm((256, 1024), BF), vm((4, 512, 512), BF),
        dma, dma, dma((4,)), dma((4,)), dma((4,)), dma, dma, dma, dma, dma, dma, dma, dma, dma,
        dma((3,)), dma((3,)), dma((4, 4)), dma((4, 4)), dma((4,)), dma((4,)), dma((5, 3)), dma((5, 3)),
        dma((4, 2)), dma((4, 2)), dma((10, 2)), dma((10, 2)), dma((10, 2)), dma((10, 2)),
        dma((3, 4)), dma((3, 4)), dma((7,)), dma((7,)),
    ]
    anywhere = pl.BlockSpec(memory_space=pl.ANY)
    hbm = pl.BlockSpec(memory_space=pltpu.HBM)
    vmem = pl.BlockSpec(memory_space=pltpu.VMEM)
    return pl.pallas_call(
        kernel,
        out_shape=(
            jax.ShapeDtypeStruct((256, 1024), BF),
            jax.ShapeDtypeStruct((256, 4096), BF),
            jax.ShapeDtypeStruct((128, 128), F32),
        ),
        in_specs=[hbm] * 4,
        out_specs=(anywhere, anywhere, vmem),
        scratch_shapes=scratch,
        compiler_params=pltpu.CompilerParams(
            collective_id=0, has_side_effects=True, vmem_limit_bytes=48 * 2**20
        ),
        cost_estimate=pl.CostEstimate(flops=6442450944, bytes_accessed=8 * 2**20, transcendentals=0),
        name="key_projection",
    )(*(pltpu.with_memory_space_constraint(v, pltpu.HBM) for v in (tokens, cotangent, quantized, scales.T)))


def solution(mesh):
    in_specs = (P(("dp", "node"), None), P(("dp", "node"), None), P("dp", None), P("dp", None))
    out_specs = (P(("dp", "node"), None), P(("dp", "node"), None), P("dp", "node"))
    return jax.shard_map(shards, mesh=mesh, in_specs=in_specs, out_specs=out_specs, check_vma=False)
```

```python
import jax
import jax.numpy as jnp
from jax import lax
from jax.experimental import pallas as pl
from jax.experimental.pallas import tpu as pltpu
from jax.sharding import PartitionSpec as P

MESH = pl.DeviceIdType.MESH
BF = jnp.bfloat16
F32 = jnp.float32


def nn(a, b):
    return lax.dot_general(a, b, (((1,), (0,)), ((), ())), preferred_element_type=F32)


def nt(a, b):
    return lax.dot_general(a, b, (((1,), (1,)), ((), ())), preferred_element_type=F32)


def kernel(
    tok, cot, codes_h, scales_h, keys_o, gi_o, gw_o,
    quantized, scales_t, tk, ct, ctt, w1, w2, s1s, s1r, dps, dpr, s2s, s2r, xo, ys, yr, yt, zs, zr, kacc, krecv, kout, gis,
    codes_l, scales_l, tok_l, tok_s, tok_r, cot_l, cot_s, cot_r, key_s, key_r, key_l, gi_l, gi_s, gi_r,
    hy_s, hy_r, hz_s, hz_r, gz_s, gz_r, gy_s, gy_r,
    s1_s, s1_q, dp_s, dp_q, s2_s, s2_q, y_s, y_q, z_s, z_q,
):
    dp, node = lax.axis_index("dp"), lax.axis_index("node")
    y, zh, c = dp // 8, (dp // 2) % 4, dp % 2
    zl, x = node // 4, node % 4
    z = zh * 2 + zl
    dirz = 2 * zl - 1

    def at(dx=0, dy=0, dz=0, dc=0):
        x2, y2, z2 = (x + dx + 4) % 4, (y + dy + 4) % 4, (z + dz + 8) % 8
        c2 = c if dc == 0 else 1 - c
        return (y2 * 8 + (z2 // 2) * 2 + c2, (z2 % 2) * 4 + x2)

    sib = at(dc=1)
    pending = []

    def send(src, dst, ss, rs, dev):
        cp = pltpu.make_async_remote_copy(src, dst, ss, rs, device_id=dev, device_id_type=MESH)
        cp.start()
        pending.append(cp)

    def arrived(dst, rs):
        pltpu.make_async_remote_copy(dst, dst, rs, rs, device_id=sib, device_id_type=MESH).wait_recv()

    def mod4(v):
        return (v + 4) % 4

    barrier = pltpu.get_barrier_semaphore()
    peers = [at(dx=1), at(dx=-1)] + [at(dy=o) for o in (1, 2, 3)] + [at(dz=j) for j in range(1, 8)] + [sib]
    for peer in peers:
        pl.semaphore_signal(barrier, inc=1, device_id=peer, device_id_type=MESH)

    def cols(yy, h):
        return pl.ds(pl.multiple_of(((yy * 4 + h) * 2 + c) * 128, 128), 128)

    def cols_sib(yy, h):
        return pl.ds(pl.multiple_of(((yy * 4 + h) * 2 + 1 - c) * 128, 128), 128)

    cp_cot = pltpu.make_async_copy(cot, ct.at[pl.ds(0, 256)], cot_l)
    cp_cot.start()
    cp_scales = pltpu.make_async_copy(scales_h, scales_t, scales_l)
    cp_scales.start()
    cp_codes = pltpu.make_async_copy(codes_h, quantized, codes_l)
    cp_codes.start()
    for i in range(4):
        yy = (y + i + 1) % 4
        for h in range(4):
            pltpu.make_async_copy(
                tok.at[:, cols(yy, h)], tk.at[yy, h, pl.ds(0, 256)], tok_l.at[i]
            ).start()

    pl.semaphore_wait(barrier, len(peers))

    send(cot, ct.at[pl.ds(256, 256)], cot_s, cot_r, sib)
    for i in range(4):
        yy = (y + i + 1) % 4
        for h in range(4):
            pltpu.make_async_remote_copy(
                tok.at[:, cols_sib(yy, h)], tk.at[yy, h, pl.ds(256, 256)],
                tok_s.at[i], tok_r.at[i], device_id=sib, device_id_type=MESH,
            ).start()

    cp_scales.wait()
    cp_codes.wait()
    for b in range(4):
        scale = jnp.transpose(jnp.broadcast_to(scales_t[b : b + 1, :], (128, 128)))
        for half in range(2):
            col = b * 256 + half * 128
            block = (quantized[:, col : col + 128].astype(F32) * scale).astype(BF)
            if col < 512:
                w1[y, zh, :, col : col + 128] = block
            else:
                w2[y, zh, :, col - 512 : col - 384] = block

    def half(flag):
        return pl.ds(pl.multiple_of(flag * 64, 64), 64)

    cross, pair = at(dz=dirz), at(dz=0 - dirz)
    near, back, far = mod4(zh + dirz), mod4(zh - dirz), mod4(zh + 2)

    def z_send(w, yy, phase, ss, rs):
        block, dev = (
            (w.at[yy, zh], cross),
            (w.at[yy, near], pair),
            (w.at[yy, back, half(1 - zl)], cross),
            (w.at[yy, far, half(zl)], pair),
        )[phase]
        send(block, block, ss.at[phase], rs.at[phase], dev)

    def z_wait(w, yy, phase, rs):
        block = (w.at[yy, near], w.at[yy, back], w.at[yy, far, half(zl)], w.at[yy, far, half(1 - zl)])[phase]
        arrived(block, rs.at[phase])

    def h_send(r, phase):
        z_send(w1, (y + r) % 4, phase, hz_s.at[r], hz_r.at[r])

    def h_pass(r, phase):
        z_wait(w1, (y + r) % 4, phase, hz_r.at[r])
        if phase < 3:
            h_send(r, phase + 1)

    def h_first(o):
        yy = mod4(y - o)
        arrived(w1.at[yy, zh], hy_r.at[o - 1])
        h_send(4 - o, 0)

    roles = (
        (zh, pl.ds(0, 128)), (near, pl.ds(0, 128)), (back, pl.ds(0, 128)), (far, half(zl)), (far, half(1 - zl)),
    )

    def g_along_y(role):
        zz, rows = roles[role]
        for o in (1, 3, 2):
            send(w2.at[y, zz, rows], w2.at[y, zz, rows], gy_s.at[role, o - 1], gy_r.at[role, o - 1], at(dy=o))

    def g_pass(phase):
        z_wait(w2, y, phase, gz_r)
        if phase < 3:
            z_send(w2, y, phase + 1, gz_s, gz_r)
        g_along_y(phase + 1)

    z_send(w2, y, 0, gz_s, gz_r)
    for o in (1, 3, 2):
        send(w1.at[y, zh], w1.at[y, zh], hy_s.at[o - 1], hy_r.at[o - 1], at(dy=o))
    h_send(0, 0)
    g_along_y(0)

    def transpose_rows(r):
        for n in range(8):
            part = ct[r * 256 : r * 256 + 256, n * 128 : n * 128 + 128]
            row = (n // 4) * 128
            ctt[n % 4, row : row + 128, r * 256 : r * 256 + 256] = jnp.transpose(part)

    cp_cot.wait()
    transpose_rows(0)
    arrived(ct.at[pl.ds(256, 256)], cot_r)
    transpose_rows(1)

    east, west = at(dx=1), at(dx=-1)
    lo, hi = pl.ds(0, 128), pl.ds(128, 128)
    xe, xw, xf = (x + 1) % 4, (x + 3) % 4, (x + 2) % 4

    def put(ref, i, rows, value):
        for q in range(4):
            ref[i, q, rows] = value[:, q * 128 : q * 128 + 128].astype(ref.dtype)

    def get(ref, i, rows):
        return jnp.concatenate([ref[i, q, rows].astype(F32) for q in range(4)], axis=1)

    top, low = slice(0, 128), slice(128, 256)

    order = (2, 1, 3, 0)

    def tokens_of(yy, q):
        return tk[yy, (zh + order[q]) % 4]

    def chunk(yy):
        return jnp.concatenate([tokens_of(yy, q) for q in range(4)], axis=1)

    def s1(i):
        yy = (y + i + 1) % 4
        pltpu.make_async_copy(tk.at[yy, :, pl.ds(0, 256)], tk.at[yy, :, pl.ds(0, 256)], tok_l.at[i]).wait()
        arrived(tk.at[yy, :, pl.ds(256, 256)], tok_r.at[i])
        put(s1s, i, slice(0, 256), nn(ctt[xf], chunk(yy)))
        send(s1s.at[i, :, lo], s1r.at[i, :, lo], s1_s.at[i, 0], s1_q.at[i, 0], east)
        send(s1s.at[i, :, hi], s1r.at[i, :, hi], s1_s.at[i, 1], s1_q.at[i, 1], west)

    def pieces(i):
        return ((i, slice(None)),) if i < 2 else tuple((4 * i - 6 + q, q) for q in range(4))

    def x_step(i):
        tokens = chunk((y + i + 1) % 4)
        right, left = nn(ctt[xe], tokens), nn(ctt[xw], tokens)
        put(dps, i, low, right[128:256])
        put(dps, i, top, left[0:128])
        arrived(s1r.at[i, :, lo], s1_q.at[i, 0])
        put(s2s, i, top, right[0:128] + get(s1r, i, top))
        arrived(s1r.at[i, :, hi], s1_q.at[i, 1])
        put(s2s, i, low, left[128:256] + get(s1r, i, low))
        for k, q in pieces(i):
            send(s2s.at[i, q, lo], s2r.at[i, q, lo], s2_s.at[k, 0], s2_q.at[k, 0], east)
            send(s2s.at[i, q, hi], s2r.at[i, q, hi], s2_s.at[k, 1], s2_q.at[k, 1], west)
            send(dps.at[i, q, hi], dpr.at[i, q, hi], dp_s.at[k, 1], dp_q.at[k, 1], east)
            send(dps.at[i, q, lo], dpr.at[i, q, lo], dp_s.at[k, 0], dp_q.at[k, 0], west)

    def x_wait(i, k, q):
        for j, rows in ((0, lo), (1, hi)):
            arrived(s2r.at[i, q, rows], s2_q.at[k, j])
            arrived(dpr.at[i, q, rows], dp_q.at[k, j])

    def x_end(i):
        total = nn(ctt[x], chunk((y + i + 1) % 4))
        if i < 2:
            x_wait(i, i, slice(None))
        for q in range(4):
            if i == 2:
                x_wait(i, 2 + q, q)
            piece = total[:, q * 128 : q * 128 + 128]
            ys[i, q] = (piece + dpr[i, q].astype(F32) + s2r[i, q].astype(F32)).astype(BF)
            send(ys.at[i, q], yr.at[i, q], y_s.at[i, q], y_q.at[i, q], at(dy=i + 1))

    def own_chunk():
        total = nn(ctt[x], chunk(y))
        for q in range(4):
            xo[q] = total[:, q * 128 : q * 128 + 128]

    def last(q):
        total = xo[q]
        x_wait(3, 6 + q, q)
        total = total + dpr[3, q].astype(F32) + s2r[3, q].astype(F32)
        for i in range(3):
            arrived(yr.at[i, q], y_q.at[i, q])
            total = total + yr[i, q].astype(F32)
        zs[q, 0] = total[0:128].astype(BF)
        zs[q, 1] = total[128:256].astype(BF)
        if q < 3:
            for t in range(2):
                dz = 2 * order[q] + t - zl
                send(zs.at[q, t], zr.at[q * 2 + zl], z_s.at[q * 2 + t], z_q.at[q * 2 + zl], at(dz=dz))
        else:
            send(zs.at[q, 1 - zl], zr.at[6], z_s.at[6], z_q.at[6], pair)
            yt[0] = total[0:128]
            yt[1] = total[128:256]

    def use_weight(p):
        tokens = jnp.concatenate([tk[p, h] for h in range(4)], axis=1)
        a, b = w1[p].reshape(512, 512), w2[p].reshape(512, 512)
        for r in range(2):
            rows = slice(r * 256, r * 256 + 256)
            gis[p, rows] = (nt(ct[rows, 0:512], a) + nt(ct[rows, 512:1024], b)).astype(BF)
        for h in range(4):
            here = pl.ds(h * 128, 128)
            pltpu.make_async_remote_copy(
                gis.at[p, pl.ds(256, 256), here], gi_o.at[:, cols(p, h)],
                gi_s, gi_r, device_id=sib, device_id_type=MESH,
            ).start()
            pltpu.make_async_copy(gis.at[p, pl.ds(0, 256), here], gi_o.at[:, cols(p, h)], gi_l).start()
        if p == 0:
            kacc[:, 0:512] = nn(tokens, a)
            kacc[:, 512:1024] = nn(tokens, b)
        else:
            kacc[:, 0:512] += nn(tokens, a)
            kacc[:, 512:1024] += nn(tokens, b)

    s1(0)
    s1(1)
    g_pass(0)
    h_first(1)
    h_first(3)
    h_pass(0, 0)
    s1(2)
    s1(3)
    g_pass(1)
    h_first(2)
    x_step(0)
    h_pass(0, 1)
    h_pass(3, 0)
    h_pass(1, 0)
    x_step(1)
    g_pass(2)
    h_pass(0, 2)
    h_pass(3, 1)
    h_pass(1, 1)
    h_pass(2, 0)
    x_step(2)
    g_pass(3)
    h_pass(3, 2)
    h_pass(1, 2)
    h_pass(2, 1)
    early = len(pending)
    x_step(3)
    h_pass(2, 2)
    x_end(0)
    x_end(1)
    h_pass(0, 3)
    h_pass(3, 3)
    h_pass(1, 3)
    h_pass(2, 3)
    for role in range(5):
        zz, rows = roles[role]
        for o in (1, 3, 2):
            arrived(w2.at[mod4(y - o), zz, rows], gy_r.at[role, o - 1])
    use_weight(0)
    use_weight(1)
    x_end(2)
    use_weight(2)
    use_weight(3)
    send(kacc.at[pl.ds(256, 256)], krecv, key_s, key_r, sib)
    own_chunk()
    for cp in pending[:early]:
        cp.wait_send()
    for i in range(4):
        pltpu.make_async_copy(tk.at[0, :, pl.ds(256, 256)], tk.at[0, :, pl.ds(256, 256)], tok_s.at[i]).wait()
    for q in range(4):
        last(q)
    arrived(krecv, key_r)
    kout[...] = (kacc[0:256] + krecv[...]).astype(BF)
    cp_key = pltpu.make_async_copy(kout, keys_o, key_l)
    cp_key.start()
    acc = yt[zl]
    for j in range(7):
        arrived(zr.at[j], z_q.at[j])
        acc = acc + zr[j].astype(F32)
    gw_o[...] = jnp.transpose(acc) * 0.00390625

    for cp in pending[early:]:
        cp.wait_send()
    wide = pl.ds(0, 2048)
    pltpu.make_async_copy(gi_o.at[:, wide], gi_o.at[:, wide], gi_l).wait()
    pltpu.make_async_copy(gi_o.at[:, wide], gi_o.at[:, wide], gi_s).wait()
    pltpu.make_async_copy(gi_o.at[:, wide], gi_o.at[:, wide], gi_r).wait()
    cp_key.wait()


def shards(tokens, cotangent, quantized, scales):
    dma = pltpu.SemaphoreType.DMA
    vm = pltpu.VMEM
    piece = (4, 4, 256, 128)
    scratch = [
        vm((128, 1024), BF), vm((4, 128), F32), vm((4, 4, 512, 128), BF), vm((512, 1024), BF), vm((4, 256, 512), BF),
        vm((4, 4, 128, 512), BF), vm((4, 4, 128, 512), BF),
        vm(piece, BF), vm(piece, BF), vm(piece, BF), vm(piece, BF), vm(piece, BF), vm(piece, BF),
        vm((4, 256, 128), F32), vm((3, 4, 256, 128), BF), vm((3, 4, 256, 128), BF),
        vm((2, 128, 128), F32), vm((4, 2, 128, 128), BF), vm((7, 128, 128), BF),
        vm((512, 1024), F32), vm((256, 1024), F32), vm((256, 1024), BF), vm((4, 512, 512), BF),
        dma, dma, dma((4,)), dma((4,)), dma((4,)), dma, dma, dma, dma, dma, dma, dma, dma, dma,
        dma((3,)), dma((3,)), dma((4, 4)), dma((4, 4)), dma((4,)), dma((4,)), dma((5, 3)), dma((5, 3)),
        dma((4, 2)), dma((4, 2)), dma((10, 2)), dma((10, 2)), dma((10, 2)), dma((10, 2)),
        dma((3, 4)), dma((3, 4)), dma((7,)), dma((7,)),
    ]
    anywhere = pl.BlockSpec(memory_space=pl.ANY)
    hbm = pl.BlockSpec(memory_space=pltpu.HBM)
    vmem = pl.BlockSpec(memory_space=pltpu.VMEM)
    return pl.pallas_call(
        kernel,
        out_shape=(
            jax.ShapeDtypeStruct((256, 1024), BF),
            jax.ShapeDtypeStruct((256, 4096), BF),
            jax.ShapeDtypeStruct((128, 128), F32),
        ),
        in_specs=[hbm] * 4,
        out_specs=(anywhere, anywhere, vmem),
        scratch_shapes=scratch,
        compiler_params=pltpu.CompilerParams(
            collective_id=0, has_side_effects=True, vmem_limit_bytes=48 * 2**20
        ),
        cost_estimate=pl.CostEstimate(flops=6442450944, bytes_accessed=8 * 2**20, transcendentals=0),
        name="key_projection",
    )(*(pltpu.with_memory_space_constraint(v, pltpu.HBM) for v in (tokens, cotangent, quantized, scales.T)))


def solution(mesh):
    in_specs = (P(("dp", "node"), None), P(("dp", "node"), None), P("dp", None), P("dp", None))
    out_specs = (P(("dp", "node"), None), P(("dp", "node"), None), P("dp", "node"))
    return jax.shard_map(shards, mesh=mesh, in_specs=in_specs, out_specs=out_specs, check_vma=False)
```
